256 devices in a mesh: rep: 8 (over y, z_hi), row: 32 (over z_lo, x, core).
Axes of the slice: x: 4, y: 4, z: 8 (z_hi: 2, z_lo: 4; z = z_hi * 4 + z_lo), core: 2. Of those that a mesh axis runs over, the one named last changes fastest.
Arguments:
- delta: bfloat16 [8, 512, 53248], P('rep', 'row'), may hold values from -6 to 6
- q_start: bfloat16 [53248, 64], P('row'), may hold values from -0.02734375 to 0.02734375
- first_moment: float32 [512, 53248], P('row', 'rep'), may hold values from -0.12 to 0.12
- second_moment: float32 [512, 53248], P('row', 'rep'), may hold values from 0.01 to 0.2
Outputs:
- update: float32 [512, 53248], P('row', 'rep')
- new_first: float32 [512, 53248], P('row', 'rep')
- new_second: float32 [512, 53248], P('row', 'rep')
- q_new: float32 [53248, 64], P(('rep', 'row'))
The draws below stay inside these ranges and needn't reach their ends.
All inputs are finite; a program needn't handle non-finite values.
Results may differ from the reference program's by a relative error of at most 0.0029.
Values may be sent and summed in bfloat16 or wider, within the bound.
No kernel may reach another device: no remote copies, remote signals or barrier semaphores. Data moves between devices by JAX's collectives and lax.ppermute only.
A program may use at most 128 MiB of HBM per device.

```python
import math
import jax
import jax.numpy as jnp
from jax import lax

NCOL = 53248
R = 64
ROWS = 512
N_REP = 8


def with_spikes(drawn, own_key, source, target, shards_of, factor):
    def block_of(dim):
        return (jnp.arange(drawn.shape[dim]) // (drawn.shape[dim] // shards_of)).reshape((-1,) + (1,) * (drawn.ndim - 1 - dim))

    near = jax.random.permutation(own_key, shards_of)[block_of(target)]
    second = (block_of(target) + shards_of // 2) % shards_of
    return jnp.where((block_of(source) == near) | (block_of(source) == second), factor * drawn, drawn)


def shard_levels(rng, extent, split, least, largest):
    gain = 1.0
    for position, parts in split:
        heights = jax.random.uniform(jax.random.fold_in(jax.random.fold_in(rng, 6), position), (parts,), jnp.float32, least / len(split), largest / len(split))
        gain = gain * jnp.repeat(jnp.exp(heights), extent[position] // parts).reshape((-1,) + (1,) * (len(extent) - 1 - position))
    return gain


def noise(key, dims, width, bound, split=(), held_as=jnp.bfloat16):
    values = width * jax.random.normal(key, dims, jnp.float32)
    if split:
        values = values * shard_levels(key, dims, split, -0.22, 0.18)
    return jnp.clip(values, -bound, bound).astype(held_as)


def gaussian_with(rng, extent, width, most, cuts, heavy, kind=jnp.bfloat16):
    array = width * jax.random.normal(rng, extent, jnp.float32)
    if cuts:
        array = array * shard_levels(rng, extent, cuts, -0.22, 0.18)
    return jnp.clip(with_spikes(array, jax.random.fold_in(rng, 3), *heavy), -most, most).astype(kind)


def setup_inputs(seed: int = 0) -> dict:
    splits = jax.random.split(jax.random.key(seed), 5)
    delta = gaussian_with(splits[0], (N_REP, ROWS, NCOL), 1.0, 6.0, ((0, 8), (1, 32)), (0, 2, 8, 2.0))
    q_start = noise(splits[1], (NCOL, R), NCOL ** -0.5, 0.02734375, ((0, 32),))
    first_moment = noise(splits[2], (ROWS, NCOL), 0.02, 0.12, ((0, 32), (1, 8)), jnp.float32)
    second_moment = jnp.clip(jnp.exp(math.log(0.2) - 2.9957323 * jax.random.uniform(splits[3], (ROWS, NCOL), jnp.float32) ** shard_levels(splits[3], (ROWS, NCOL), ((0, 32), (1, 8)), -0.2, 0.2)), 0.01, 0.2)
    return dict(delta=delta, q_start=q_start, first_moment=first_moment, second_moment=second_moment)


beta_first = 0.9
beta_second = 0.95
fix_first = 1.0 / (1.0 - 0.9 ** 10)
fix_second = 1.0 / (1.0 - 0.95 ** 10)
epsilon = 1e-08

def reference(delta, q_start, first_moment, second_moment):
    p_sum = jnp.zeros((ROWS, R), jnp.float32)
    for replica in range(N_REP):
        p_sum = p_sum + jnp.dot(delta[replica].astype(jnp.float32), q_start.astype(jnp.float32), preferred_element_type=jnp.float32)
    gram_matrix = jnp.dot(p_sum.T.astype(jnp.float32), p_sum.astype(jnp.float32), precision=lax.Precision.HIGHEST, preferred_element_type=jnp.float32)
    chol_lower = jnp.linalg.cholesky(gram_matrix)
    p_orth = jax.scipy.linalg.solve_triangular(chol_lower, p_sum.T, lower=True).T.astype(jnp.bfloat16)
    q_total = jnp.zeros((NCOL, R), jnp.float32)
    square_total = jnp.zeros((ROWS, NCOL), jnp.float32)
    for replica in range(N_REP):
        q_total = q_total + lax.dot_general(delta[replica].astype(jnp.float32), p_orth.astype(jnp.float32), (((0,), (0,)), ((), ())), preferred_element_type=jnp.float32)
        square_total = square_total + jnp.square(delta[replica].astype(jnp.float32))
    q_new = q_total / N_REP
    mean_square = square_total / N_REP
    approx = jnp.dot(p_orth.astype(jnp.float32), q_new.T.astype(jnp.float32), precision=lax.Precision.HIGHEST, preferred_element_type=jnp.float32)
    new_first = beta_first * first_moment + (1.0 - beta_first) * approx
    new_second = beta_second * second_moment + (1.0 - beta_second) * mean_square
    update = new_first * fix_first / (jnp.sqrt(new_second * fix_second) + epsilon)
    return (update, new_first, new_second, q_new)
```

```python
import jax
import jax.numpy as jnp
from jax import lax
from jax.experimental import pallas as pl
from jax.experimental.pallas import tpu as pltpu
from jax.sharding import Mesh, PartitionSpec as P

beta_first = 0.9
beta_second = 0.95
fix_first = 1.0 / (1.0 - 0.9**10)
fix_second = 1.0 / (1.0 - 0.95**10)
epsilon = 1e-08

NAMES = ("y", "zh", "zl", "x", "c")
SIZES = (4, 2, 4, 4, 2)
REP = ("y", "zh")
ROW = ("zl", "x", "c")
REPS = 8
HIGHEST = lax.Precision.HIGHEST
f32 = jnp.float32
bf16 = jnp.bfloat16


def swap(x, axis, bits):
    return lax.ppermute(x, axis, [(i, i ^ bits) for i in range(lax.axis_size(axis))])


def in_order(blocks, place):
    n = len(blocks)
    bit = 1
    while bit < n:
        set_ = (place & bit) != 0
        blocks = [jnp.where(set_, blocks[k ^ bit], blocks[k]) for k in range(n)]
        bit *= 2
    return blocks


def dot(a, b, contract, precision=None):
    return lax.dot_general(a, b, (contract, ((), ())), precision=precision, preferred_element_type=f32)


def p_kernel(starts, *refs):
    shards, blocks, out = refs[:8], refs[8:12], refs[12]
    rank, span = shards[0].shape
    rows = blocks[0].shape[0]
    total = jnp.zeros((4 * rows, rank), f32)
    for k in range(8):
        at = pl.ds(pl.multiple_of(starts[k], 128), span)
        lhs = jnp.concatenate([b[:, at] for b in blocks], axis=0)
        total = total + dot(lhs, shards[k][...], ((1,), (1,)))
    p = total[:rows] + total[rows : 2 * rows] + total[2 * rows : 3 * rows] + total[3 * rows :]
    out[...] = jnp.concatenate([p, jnp.zeros((rows, 128 - rank), f32)], axis=1)


def p_of(starts, shards, blocks):
    vmem = pl.BlockSpec(memory_space=pltpu.VMEM)
    return pl.pallas_call(
        p_kernel,
        out_shape=jax.ShapeDtypeStruct((blocks[0].shape[0], 128), f32),
        in_specs=[pl.BlockSpec(memory_space=pltpu.SMEM)] + [vmem] * 12,
        out_specs=vmem,
        compiler_params=pltpu.CompilerParams(vmem_limit_bytes=32 * 2**20),
        cost_estimate=pl.CostEstimate(flops=2**27, bytes_accessed=3 * 2**20, transcendentals=0),
        name="p_kernel",
    )(starts, *shards, *blocks)


def mid_kernel(p_ref, came, q_out, approx_out):
    half, rank = came.shape[0] // 2, 64
    span = q_out.shape[1]
    p = p_ref[:, :rank]
    gram = dot(p, p, ((0,), (0,)), HIGHEST)
    row = lax.broadcasted_iota(jnp.int32, (rank, rank), 0)
    col = lax.broadcasted_iota(jnp.int32, (rank, rank), 1)
    a = jnp.concatenate([gram, jnp.where(row == col, 1.0, 0.0).astype(f32)], axis=1)
    below = lax.broadcasted_iota(jnp.int32, (rank, 2 * rank), 0)
    scale = jnp.zeros((rank, 1), f32)
    place = lax.broadcasted_iota(jnp.int32, (rank, 1), 0)
    for j in range(rank):
        pivot = a[j : j + 1, :]
        d = pivot[:, j : j + 1]
        factor = jnp.where(below > j, jnp.broadcast_to(a[:, j : j + 1], (rank, 2 * rank)), 0.0)
        a = a - factor * (pivot * (1.0 / d))
        scale = jnp.where(place == j, d, scale)
    inverse = a[:, rank:] * (1.0 / jnp.sqrt(scale))
    p_orth = dot(p, inverse, ((1,), (1,)), HIGHEST).astype(bf16)
    d_cols = came[:, :span]
    q_t = (dot(p_orth, d_cols[:half], ((0,), (0,))) + dot(p_orth, d_cols[half:], ((0,), (0,)))) / REPS
    q_out[...] = q_t
    approx_out[...] = dot(p_orth.astype(f32), q_t, ((1,), (0,)), HIGHEST).astype(bf16)


def middle(p_sum, came, span):
    vmem = pl.BlockSpec(memory_space=pltpu.VMEM)
    rows = came.shape[0]
    return pl.pallas_call(
        mid_kernel,
        out_shape=(
            jax.ShapeDtypeStruct((64, span), f32),
            jax.ShapeDtypeStruct((rows // 2, span), bf16),
        ),
        in_specs=[vmem, vmem],
        out_specs=(vmem, vmem),
        compiler_params=pltpu.CompilerParams(vmem_limit_bytes=32 * 2**20),
        cost_estimate=pl.CostEstimate(flops=2**33, bytes_accessed=2**20, transcendentals=0),
        name="mid_kernel",
    )(p_sum, came)


def body(delta, q_start, first_moment, second_moment):
    own = delta[0]
    rows, cols = own.shape
    rank = q_start.shape[1]
    wide = cols // 4
    block = cols // REPS
    narrow = block // 32
    y = lax.axis_index("y")
    zh = lax.axis_index("zh")

    x, c = lax.axis_index("x"), lax.axis_index("c")

    def part(k):
        return lax.dynamic_slice(own, (0, (y ^ k) * wide), (rows, wide))

    with jax.named_scope("q_z"):
        q_t = q_start.T
        quarter = rank // 4
        shard = jnp.concatenate(
            [
                lax.ppermute(
                    q_t[quarter * s : quarter * (s + 1)],
                    ("y", "zl"),
                    [(a * 4 + b, b * 4 + (a ^ s)) for a in range(4) for b in range(4)],
                )
                for s in range(4)
            ],
            axis=0,
        )
    with jax.named_scope("delta_y"):
        near = [swap(part(k), "y", k) for k in (1, 3)]
    shard, near = lax.optimization_barrier((shard, near))
    far = part(2)
    with jax.named_scope("q_x"):
        shards = [shard] + [swap(shard, "x", k) for k in (1, 3, 2)]
    with jax.named_scope("delta_y2"):
        far = swap(far, "y", 2)
    shards, far = lax.optimization_barrier((shards, far))
    with jax.named_scope("q_c"):
        shards = shards + [swap(s, "c", 1) for s in shards]
    arrived = [part(0), far] + near
    with jax.named_scope("p_part"):
        starts = jnp.stack([((x ^ k) * 2 + (c ^ i)) * (wide // 8) for i in (0, 1) for k in (0, 1, 3, 2)])
        p_part = p_of(starts, shards, arrived)
    with jax.named_scope("sums"):
        vals = [a.astype(f32) for a in arrived]
        d_part = sum(vals)
        s_part = sum(jnp.square(v) for v in vals)

    with jax.named_scope("d_cols"):
        d_send = d_part.astype(bf16).reshape(rows, 64, narrow).transpose(1, 0, 2)
        came = lax.all_to_all(d_send, ("zh",) + ROW, 0, 0, tiled=True)
    with jax.named_scope("p_y"):
        p_part = p_part + (swap(p_part, "y", 1) + swap(p_part, "y", 3)) + swap(p_part, "y", 2)
    with jax.named_scope("p_zh"):
        p_part = p_part + swap(p_part, "zh", 1)
    with jax.named_scope("p_zl"):
        p_z = jnp.stack(in_order([p_part] + [swap(p_part, "zl", k) for k in (1, 2, 3)], lax.axis_index("zl")))
    with jax.named_scope("squares"):
        at = [(0, half * block) for half in (zh, 1 - zh)]
        s_keep, s_send = [lax.dynamic_slice(s_part, start, (rows, block)) for start in at]
        s_send, p_z = lax.optimization_barrier((s_send.astype(bf16), p_z))
        s_came = swap(s_send, "zh", 1)
    with jax.named_scope("p_xc"):
        p_c = jnp.stack(in_order([p_z, swap(p_z, "c", 1)], c), axis=1)
        p_c, came = lax.optimization_barrier((p_c, came))
        p_xc = [p_c] + [swap(p_c, "x", k) for k in (1, 2, 3)]
        p_sum = jnp.stack(in_order(p_xc, x), axis=1).reshape(32 * rows, 128)
    with jax.named_scope("middle"):
        q_t, approx_cols = middle(p_sum, came.reshape(64 * rows, narrow), narrow)
        q_new = q_t.T
    with jax.named_scope("second"):
        approx_cols, s_came = lax.optimization_barrier((approx_cols, s_came))
        mean_square = (s_keep + s_came.astype(f32)) / REPS
        new_second = beta_second * second_moment + (1.0 - beta_second) * mean_square
    with jax.named_scope("approx"):
        approx = lax.all_to_all(
            approx_cols.reshape(32, rows, narrow), ROW, 0, 0, tiled=True
        )
        approx = approx.transpose(1, 0, 2).reshape(rows, block).astype(f32)

    new_first = beta_first * first_moment + (1.0 - beta_first) * approx
    update = new_first * fix_first / (jnp.sqrt(new_second * fix_second) + epsilon)
    return (update, new_first, new_second, q_new)


def solution(mesh):
    fine = Mesh(mesh.devices.reshape(SIZES), NAMES)
    in_specs = (P(REP, ROW, None), P(ROW, None), P(ROW, REP), P(ROW, REP))
    out_specs = (P(ROW, REP), P(ROW, REP), P(ROW, REP), P(REP + ROW, None))
    return jax.shard_map(body, mesh=fine, in_specs=in_specs, out_specs=out_specs, check_vma=False)
```

```python
import jax
import jax.numpy as jnp
from jax import lax
from jax.experimental import pallas as pl
from jax.experimental.pallas import tpu as pltpu
from jax.sharding import Mesh, PartitionSpec as P

beta_first = 0.9
beta_second = 0.95
fix_first = 1.0 / (1.0 - 0.9**10)
fix_second = 1.0 / (1.0 - 0.95**10)
epsilon = 1e-08

NAMES = ("y", "zh", "zl", "x", "c")
SIZES = (4, 2, 4, 4, 2)
REP = ("y", "zh")
ROW = ("zl", "x", "c")
REPS = 8
HIGHEST = lax.Precision.HIGHEST
f32 = jnp.float32
bf16 = jnp.bfloat16


def swap(x, axis, bits):
    return lax.ppermute(x, axis, [(i, i ^ bits) for i in range(lax.axis_size(axis))])


def in_order(blocks, place):
    n = len(blocks)
    bit = 1
    while bit < n:
        set_ = (place & bit) != 0
        blocks = [jnp.where(set_, blocks[k ^ bit], blocks[k]) for k in range(n)]
        bit *= 2
    return blocks


def dot(a, b, contract, precision=None):
    return lax.dot_general(a, b, (contract, ((), ())), precision=precision, preferred_element_type=f32)


def split_kernel(zh, own, give, keep):
    block = give.shape[2]
    mine, other = pl.multiple_of(zh[0] * block, 128), pl.multiple_of((1 - zh[0]) * block, 128)
    for k in range(4):
        give[k] = own[:, pl.ds(2 * k * block + other, block)]
        keep[k] = own[:, pl.ds(2 * k * block + mine, block)]


def split(zh, own):
    vmem = pl.BlockSpec(memory_space=pltpu.VMEM)
    half = jax.ShapeDtypeStruct((4, own.shape[0], own.shape[1] // 8), own.dtype)
    return pl.pallas_call(
        split_kernel,
        out_shape=(half, half),
        in_specs=[pl.BlockSpec(memory_space=pltpu.SMEM), vmem],
        out_specs=(vmem, vmem),
        compiler_params=pltpu.CompilerParams(vmem_limit_bytes=32 * 2**20),
        cost_estimate=pl.CostEstimate(flops=0, bytes_accessed=2**22, transcendentals=0),
        name="split_kernel",
    )(zh.reshape(1), own)


def p_kernel(places, *refs):
    shards, first, second, out = refs[:8], refs[8], refs[9], refs[10]
    rank, span = shards[0].shape
    rows = first.shape[1]
    total = jnp.zeros((4 * rows, rank), f32)
    for k in range(8):
        at = pl.ds(pl.multiple_of(places[1, k], 128), span)
        late = places[0, k] != 0
        lhs = jnp.where(late, second[:, :, at], first[:, :, at]).reshape(4 * rows, span)
        total = total + dot(lhs, shards[k][...], ((1,), (1,)))
    p = total[:rows] + total[rows : 2 * rows] + total[2 * rows : 3 * rows] + total[3 * rows :]
    out[...] = jnp.concatenate([p, jnp.zeros((rows, 128 - rank), f32)], axis=1)


def p_of(places, shards, first, second):
    vmem = pl.BlockSpec(memory_space=pltpu.VMEM)
    return pl.pallas_call(
        p_kernel,
        out_shape=jax.ShapeDtypeStruct((first.shape[1], 128), f32),
        in_specs=[pl.BlockSpec(memory_space=pltpu.SMEM)] + [vmem] * 10,
        out_specs=vmem,
        compiler_params=pltpu.CompilerParams(vmem_limit_bytes=32 * 2**20),
        cost_estimate=pl.CostEstimate(flops=2**27, bytes_accessed=3 * 2**20, transcendentals=0),
        name="p_kernel",
    )(places, *shards, first, second)


def inverse_factor(gram):
    n = gram.shape[0]
    row = lax.broadcasted_iota(jnp.int32, (n, 2 * n), 0)
    col = lax.broadcasted_iota(jnp.int32, (n, 2 * n), 1)
    a = jnp.concatenate([gram, gram], axis=1)
    a = jnp.where(col < n, a, jnp.where(col == row + n, 1.0, 0.0))
    rows = lax.broadcasted_iota(jnp.int32, (n, 1), 0)
    scale = jnp.zeros((n, 1), f32)
    for j in range(0, n, 4):
        r = [a[j + i : j + i + 1, :] for i in range(4)]
        c = [jnp.broadcast_to(a[:, j + i : j + i + 1], (n, 2 * n)) for i in range(4)]
        g = [[jnp.broadcast_to(r[i][:, j + k : j + k + 1], (1, 2 * n)) for k in range(4)] for i in range(4)]
        for i in range(4):
            inv = 1.0 / g[i][i]
            scale = jnp.where(rows == j + i, g[i][i][:, :1], scale)
            rs = r[i] * inv
            for k in range(i + 1, 4):
                f = g[i][k] * inv
                r[k] = r[k] - f * r[i]
                c[k] = c[k] - f * c[i]
                for l in range(k, 4):
                    g[k][l] = g[k][l] - f * g[i][l]
            a = a - jnp.where(row > j + i, c[i], 0.0) * rs
    return a[:, n:] * (1.0 / jnp.sqrt(scale))


def mid_kernel(p_ref, came, q_out, approx_out):
    half, rank = came.shape[0], 64
    pairs = p_ref[...].reshape(16, half // 32, 2 * rank)
    p = jnp.concatenate([pairs[:, :, :rank], pairs[:, :, rank:]], axis=1).reshape(half, rank)
    inverse = inverse_factor(dot(p, p, ((0,), (0,)), HIGHEST))
    p_orth = dot(p, inverse, ((1,), (1,)), HIGHEST).astype(bf16)
    q_t = dot(p_orth, came[...], ((0,), (0,))) / REPS
    q_out[...] = q_t
    approx_out[...] = dot(p_orth.astype(f32), q_t, ((1,), (0,)), HIGHEST).astype(bf16)


def middle(p_sum, came, span):
    vmem = pl.BlockSpec(memory_space=pltpu.VMEM)
    rows = came.shape[0]
    return pl.pallas_call(
        mid_kernel,
        out_shape=(
            jax.ShapeDtypeStruct((64, span), f32),
            jax.ShapeDtypeStruct((rows, span), bf16),
        ),
        in_specs=[vmem, vmem],
        out_specs=(vmem, vmem),
        compiler_params=pltpu.CompilerParams(vmem_limit_bytes=32 * 2**20),
        cost_estimate=pl.CostEstimate(flops=2**33, bytes_accessed=2**20, transcendentals=0),
        name="mid_kernel",
    )(p_sum, came)


def body(delta, q_start, first_moment, second_moment):
    own = delta[0]
    rows, cols = own.shape
    rank = q_start.shape[1]
    wide = cols // 4
    block = cols // REPS
    narrow = block // 32
    y = lax.axis_index("y")
    zh = lax.axis_index("zh")

    x, c = lax.axis_index("x"), lax.axis_index("c")

    def along_y(a):
        return lax.all_to_all(a, "y", 0, 0, tiled=True)

    give, keep = split(zh, own)

    with jax.named_scope("q_z"):
        q_t = q_start.T
        quarter = rank // 4
        shard = jnp.concatenate(
            [
                lax.ppermute(
                    q_t[quarter * s : quarter * (s + 1)],
                    ("y", "zl"),
                    [(a * 4 + b, b * 4 + (a ^ s)) for a in range(4) for b in range(4)],
                )
                for s in range(4)
            ],
            axis=0,
        )
    with jax.named_scope("delta_give"):
        give = along_y(give)
    shard, give, keep = lax.optimization_barrier((shard, give, keep))
    with jax.named_scope("q_x"):
        shards = [shard] + [swap(shard, "x", k) for k in (1, 3, 2)]
    with jax.named_scope("delta_keep"):
        keep = along_y(keep)
    with jax.named_scope("sums_give"):
        vals = give.astype(f32)
        sums = jnp.stack([jnp.sum(vals, axis=0), jnp.sum(jnp.square(vals), axis=0)]).astype(bf16)
    with jax.named_scope("sums_zh"):
        d_came, s_came = swap(sums, "zh", 1)
    shards, keep = lax.optimization_barrier((shards, keep))
    with jax.named_scope("q_c"):
        shards = shards + [swap(s, "c", 1) for s in shards]
    with jax.named_scope("p_part"):
        at = [((x ^ k) * 2 + (c ^ i)) * (wide // 8) for i in (0, 1) for k in (0, 1, 3, 2)]
        late = [jnp.where(a >= block, 1, 0) == zh for a in at]
        places = jnp.stack([jnp.stack(late).astype(jnp.int32), jnp.stack(at) % block])
        p_part = p_of(places, shards, give, keep)
    with jax.named_scope("sums_keep"):
        vals = keep.astype(f32)
        d_keep = jnp.sum(vals, axis=0)
        s_keep = jnp.sum(jnp.square(vals), axis=0)

    with jax.named_scope("p_y"):
        p_part = p_part + (swap(p_part, "y", 1) + swap(p_part, "y", 3)) + swap(p_part, "y", 2)
    with jax.named_scope("p_zh"):
        p_part = p_part + swap(p_part, "zh", 1)
        p_part, d_came = lax.optimization_barrier((p_part, d_came))
    with jax.named_scope("d_cols"):
        d_rows = (d_keep + d_came.astype(f32)).astype(bf16)
        d_rows = d_rows.reshape(rows, 32, narrow).transpose(1, 0, 2)
        came = lax.all_to_all(d_rows, ROW, 0, 0, tiled=True)
    with jax.named_scope("p_xc"):
        other = swap(p_part, "c", 1)
        pair = jnp.where(c == 0, p_part[:, :rank], other[:, :rank]), jnp.where(c == 0, other[:, :rank], p_part[:, :rank])
        pair = jnp.concatenate(pair, axis=1)
        p_x = jnp.stack(in_order([pair] + [swap(pair, "x", k) for k in (1, 2, 3)], x))
    with jax.named_scope("p_zl"):
        p_x, came = lax.optimization_barrier((p_x, came))
        p_z = [p_x] + [swap(p_x, "zl", k) for k in (1, 2, 3)]
        p_sum = jnp.stack(in_order(p_z, lax.axis_index("zl"))).reshape(16 * rows, 2 * rank)
    with jax.named_scope("second"):
        mean_square = (s_keep + s_came.astype(f32)) / REPS
        new_second = beta_second * second_moment + (1.0 - beta_second) * mean_square
        below = jnp.sqrt(new_second * fix_second) + epsilon
        came, new_second, below = lax.optimization_barrier((came, new_second, below))
    with jax.named_scope("middle"):
        q_t, approx_cols = middle(p_sum, came.reshape(32 * rows, narrow), narrow)
        q_new = q_t.T
    with jax.named_scope("approx"):
        approx = lax.all_to_all(
            approx_cols.reshape(32, rows, narrow), ROW, 0, 0, tiled=True
        )
        approx = approx.transpose(1, 0, 2).reshape(rows, block).astype(f32)

    new_first = beta_first * first_moment + (1.0 - beta_first) * approx
    update = new_first * fix_first / below
    return (update, new_first, new_second, q_new)


def solution(mesh):
    fine = Mesh(mesh.devices.reshape(SIZES), NAMES)
    in_specs = (P(REP, ROW, None), P(ROW, None), P(ROW, REP), P(ROW, REP))
    out_specs = (P(ROW, REP), P(ROW, REP), P(ROW, REP), P(REP + ROW, None))
    return jax.shard_map(body, mesh=fine, in_specs=in_specs, out_specs=out_specs, check_vma=False)
```

```python
import jax
import jax.numpy as jnp
from jax import lax
from jax.experimental import pallas as pl
from jax.experimental.pallas import tpu as pltpu
from jax.sharding import Mesh, PartitionSpec as P

beta_first = 0.9
beta_second = 0.95
fix_first = 1.0 / (1.0 - 0.9**10)
fix_second = 1.0 / (1.0 - 0.95**10)
epsilon = 1e-08

NAMES = ("y", "zh", "zl", "x", "c")
SIZES = (4, 2, 4, 4, 2)
REP = ("y", "zh")
ROW = ("zl", "x", "c")
REPS = 8
HIGHEST = lax.Precision.HIGHEST
f32 = jnp.float32
bf16 = jnp.bfloat16


def swap(x, axis, bits):
    return lax.ppermute(x, axis, [(i, i ^ bits) for i in range(lax.axis_size(axis))])


def in_order(blocks, place):
    n = len(blocks)
    bit = 1
    while bit < n:
        set_ = (place & bit) != 0
        blocks = [jnp.where(set_, blocks[k ^ bit], blocks[k]) for k in range(n)]
        bit *= 2
    return blocks


def dot(a, b, contract, precision=None):
    return lax.dot_general(a, b, (contract, ((), ())), precision=precision, preferred_element_type=f32)


def split_kernel(zh, own, give, keep):
    block = give.shape[2]
    mine, other = pl.multiple_of(zh[0] * block, 128), pl.multiple_of((1 - zh[0]) * block, 128)
    for k in range(4):
        give[k] = own[:, pl.ds(2 * k * block + other, block)]
        keep[k] = own[:, pl.ds(2 * k * block + mine, block)]


def split(zh, own):
    vmem = pl.BlockSpec(memory_space=pltpu.VMEM)
    half = jax.ShapeDtypeStruct((4, own.shape[0], own.shape[1] // 8), own.dtype)
    return pl.pallas_call(
        split_kernel,
        out_shape=(half, half),
        in_specs=[pl.BlockSpec(memory_space=pltpu.SMEM), vmem],
        out_specs=(vmem, vmem),
        compiler_params=pltpu.CompilerParams(vmem_limit_bytes=32 * 2**20),
        cost_estimate=pl.CostEstimate(flops=0, bytes_accessed=2**22, transcendentals=0),
        name="split_kernel",
    )(zh.reshape(1), own)


def p_kernel(places, *refs):
    shards, first, second, out = refs[:8], refs[8], refs[9], refs[10]
    rank, span = shards[0].shape
    rows = first.shape[1]
    total = jnp.zeros((4 * rows, rank), f32)
    for k in range(8):
        at = pl.ds(pl.multiple_of(places[1, k], 128), span)
        late = places[0, k] != 0
        lhs = jnp.where(late, second[:, :, at], first[:, :, at]).reshape(4 * rows, span)
        total = total + dot(lhs, shards[k][...], ((1,), (1,)))
    p = total[:rows] + total[rows : 2 * rows] + total[2 * rows : 3 * rows] + total[3 * rows :]
    out[...] = jnp.concatenate([p, jnp.zeros((rows, 128 - rank), f32)], axis=1)


def p_of(places, shards, first, second):
    vmem = pl.BlockSpec(memory_space=pltpu.VMEM)
    return pl.pallas_call(
        p_kernel,
        out_shape=jax.ShapeDtypeStruct((first.shape[1], 128), f32),
        in_specs=[pl.BlockSpec(memory_space=pltpu.SMEM)] + [vmem] * 10,
        out_specs=vmem,
        compiler_params=pltpu.CompilerParams(vmem_limit_bytes=32 * 2**20),
        cost_estimate=pl.CostEstimate(flops=2**27, bytes_accessed=3 * 2**20, transcendentals=0),
        name="p_kernel",
    )(places, *shards, first, second)


def inverse_factor(gram):
    n = gram.shape[0]
    row = lax.broadcasted_iota(jnp.int32, (n, 2 * n), 0)
    col = lax.broadcasted_iota(jnp.int32, (n, 2 * n), 1)
    a = jnp.concatenate([gram, gram], axis=1)
    a = jnp.where(col < n, a, jnp.where(col == row + n, 1.0, 0.0))
    rows = lax.broadcasted_iota(jnp.int32, (n, 1), 0)
    scale = jnp.zeros((n, 1), f32)
    for j in range(0, n, 4):
        r = [a[j + i : j + i + 1, :] for i in range(4)]
        c = [jnp.broadcast_to(a[:, j + i : j + i + 1], (n, 2 * n)) for i in range(4)]
        g = [[jnp.broadcast_to(r[i][:, j + k : j + k + 1], (1, 2 * n)) for k in range(4)] for i in range(4)]
        for i in range(4):
            inv = 1.0 / g[i][i]
            scale = jnp.where(rows == j + i, g[i][i][:, :1], scale)
            rs = r[i] * inv
            for k in range(i + 1, 4):
                f = g[i][k] * inv
                r[k] = r[k] - f * r[i]
                c[k] = c[k] - f * c[i]
                for l in range(k, 4):
                    g[k][l] = g[k][l] - f * g[i][l]
            a = a - jnp.where(row > j + i, c[i], 0.0) * rs
    return a[:, n:] * (1.0 / jnp.sqrt(scale))


def mid_kernel(came, q_out, approx_out):
    rank, span = q_out.shape
    p = came[:, 256 : 256 + rank].astype(f32) + came[:, 256 + rank :].astype(f32)
    inverse = inverse_factor(dot(p, p, ((0,), (0,)), HIGHEST))
    p_orth = dot(p, inverse, ((1,), (1,)), HIGHEST).astype(bf16)
    q_t = dot(p_orth, came[:, :span], ((0,), (0,))) / REPS
    q_out[...] = q_t
    approx_out[...] = dot(p_orth.astype(f32), q_t, ((1,), (0,)), HIGHEST).astype(bf16)


def middle(came, span):
    vmem = pl.BlockSpec(memory_space=pltpu.VMEM)
    rows = came.shape[0]
    return pl.pallas_call(
        mid_kernel,
        out_shape=(
            jax.ShapeDtypeStruct((64, span), f32),
            jax.ShapeDtypeStruct((rows, span), bf16),
        ),
        in_specs=[vmem],
        out_specs=(vmem, vmem),
        compiler_params=pltpu.CompilerParams(vmem_limit_bytes=32 * 2**20),
        cost_estimate=pl.CostEstimate(flops=2**33, bytes_accessed=2**20, transcendentals=0),
        name="mid_kernel",
    )(came)


def body(delta, q_start, first_moment, second_moment):
    own = delta[0]
    rows, cols = own.shape
    rank = q_start.shape[1]
    wide = cols // 4
    block = cols // REPS
    narrow = block // 32
    y = lax.axis_index("y")
    zh = lax.axis_index("zh")

    x, c = lax.axis_index("x"), lax.axis_index("c")

    def along_y(a):
        return lax.all_to_all(a, "y", 0, 0, tiled=True)

    give, keep = split(zh, own)

    with jax.named_scope("q_z"):
        q_t = q_start.T
        quarter = rank // 4
        shard = jnp.concatenate(
            [
                lax.ppermute(
                    q_t[quarter * s : quarter * (s + 1)],
                    ("y", "zl"),
                    [(a * 4 + b, b * 4 + (a ^ s)) for a in range(4) for b in range(4)],
                )
                for s in range(4)
            ],
            axis=0,
        )
    with jax.named_scope("delta_give"):
        give = along_y(give)
    shard, give, keep = lax.optimization_barrier((shard, give, keep))
    with jax.named_scope("q_x"):
        shards = [shard] + [swap(shard, "x", k) for k in (1, 3, 2)]
    with jax.named_scope("delta_keep"):
        keep = along_y(keep)
    with jax.named_scope("sums_give"):
        vals = give.astype(f32)
        sums = jnp.stack([jnp.sum(vals, axis=0), jnp.sum(jnp.square(vals), axis=0)]).astype(bf16)
    with jax.named_scope("sums_zh"):
        d_came, s_came = swap(sums, "zh", 1)
    shards, keep = lax.optimization_barrier((shards, keep))
    with jax.named_scope("q_c"):
        shards = shards + [swap(s, "c", 1) for s in shards]
    with jax.named_scope("p_part"):
        at = [((x ^ k) * 2 + (c ^ i)) * (wide // 8) for i in (0, 1) for k in (0, 1, 3, 2)]
        late = [jnp.where(a >= block, 1, 0) == zh for a in at]
        places = jnp.stack([jnp.stack(late).astype(jnp.int32), jnp.stack(at) % block])
        p_part = p_of(places, shards, give, keep)
    with jax.named_scope("sums_keep"):
        vals = keep.astype(f32)
        d_keep = jnp.sum(vals, axis=0)
        s_keep = jnp.sum(jnp.square(vals), axis=0)

    with jax.named_scope("p_y"):
        p_part = p_part + (swap(p_part, "y", 1) + swap(p_part, "y", 3)) + swap(p_part, "y", 2)
    with jax.named_scope("p_zh"):
        p_part = p_part + swap(p_part, "zh", 1)
        p_part, d_came = lax.optimization_barrier((p_part, d_came))
    with jax.named_scope("send"):
        d_rows = (d_keep + d_came.astype(f32)).astype(bf16)
        d_rows = d_rows.reshape(rows, 32, narrow).transpose(1, 0, 2)
        d_rows = jnp.pad(d_rows, ((0, 0), (0, 0), (0, 256 - narrow)))
        p_rows = p_part[:, :rank]
        high = lax.reduce_precision(p_rows, 8, 7)
        p_rows = jnp.concatenate([high, p_rows - high], axis=1).astype(bf16)
        p_rows = jnp.broadcast_to(p_rows[None], (32, rows, 2 * rank))
        came = lax.all_to_all(jnp.concatenate([d_rows, p_rows], axis=2), ROW, 0, 0, tiled=True)
    with jax.named_scope("second"):
        mean_square = (s_keep + s_came.astype(f32)) / REPS
        new_second = beta_second * second_moment + (1.0 - beta_second) * mean_square
        below = jnp.sqrt(new_second * fix_second) + epsilon
        came, new_second, below = lax.optimization_barrier((came, new_second, below))
    with jax.named_scope("middle"):
        q_t, approx_cols = middle(came.reshape(32 * rows, 256 + 2 * rank), narrow)
        q_new = q_t.T
    with jax.named_scope("approx"):
        approx = lax.all_to_all(
            approx_cols.reshape(32, rows, narrow), ROW, 0, 0, tiled=True
        )
        approx = approx.transpose(1, 0, 2).reshape(rows, block).astype(f32)

    new_first = beta_first * first_moment + (1.0 - beta_first) * approx
    update = new_first * fix_first / below
    return (update, new_first, new_second, q_new)


def solution(mesh):
    fine = Mesh(mesh.devices.reshape(SIZES), NAMES)
    in_specs = (P(REP, ROW, None), P(ROW, None), P(ROW, REP), P(ROW, REP))
    out_specs = (P(ROW, REP), P(ROW, REP), P(ROW, REP), P(REP + ROW, None))
    return jax.shard_map(body, mesh=fine, in_specs=in_specs, out_specs=out_specs, check_vma=False)
```

```python
import jax
import jax.numpy as jnp
from jax import lax
from jax.experimental import pallas as pl
from jax.experimental.pallas import tpu as pltpu
from jax.sharding import Mesh, PartitionSpec as P

beta_first = 0.9
beta_second = 0.95
fix_first = 1.0 / (1.0 - 0.9**10)
fix_second = 1.0 / (1.0 - 0.95**10)
epsilon = 1e-08

NAMES = ("y", "zh", "zl", "x", "c")
SIZES = (4, 2, 4, 4, 2)
REP = ("y", "zh")
ROW = ("zl", "x", "c")
REPS = 8
HIGHEST = lax.Precision.HIGHEST
f32 = jnp.float32
bf16 = jnp.bfloat16


def swap(x, axis, bits):
    return lax.ppermute(x, axis, [(i, i ^ bits) for i in range(lax.axis_size(axis))])


def in_order(blocks, place):
    n = len(blocks)
    bit = 1
    while bit < n:
        set_ = (place & bit) != 0
        blocks = [jnp.where(set_, blocks[k ^ bit], blocks[k]) for k in range(n)]
        bit *= 2
    return blocks


def dot(a, b, contract, precision=None):
    return lax.dot_general(a, b, (contract, ((), ())), precision=precision, preferred_element_type=f32)


def split_kernel(zh, own, give, keep):
    block = give.shape[2]
    mine, other = pl.multiple_of(zh[0] * block, 128), pl.multiple_of((1 - zh[0]) * block, 128)
    for k in range(4):
        give[k] = own[:, pl.ds(2 * k * block + other, block)]
        keep[k] = own[:, pl.ds(2 * k * block + mine, block)]


def split(zh, own):
    vmem = pl.BlockSpec(memory_space=pltpu.VMEM)
    half = jax.ShapeDtypeStruct((4, own.shape[0], own.shape[1] // 8), own.dtype)
    return pl.pallas_call(
        split_kernel,
        out_shape=(half, half),
        in_specs=[pl.BlockSpec(memory_space=pltpu.SMEM), vmem],
        out_specs=(vmem, vmem),
        compiler_params=pltpu.CompilerParams(vmem_limit_bytes=32 * 2**20),
        cost_estimate=pl.CostEstimate(flops=0, bytes_accessed=2**22, transcendentals=0),
        name="split_kernel",
    )(zh.reshape(1), own)


def p_kernel(places, *refs):
    shards, first, second, out = refs[:8], refs[8], refs[9], refs[10]
    rank, span = shards[0].shape
    rows = first.shape[1]
    total = jnp.zeros((4 * rows, rank), f32)
    for k in range(8):
        at = pl.ds(pl.multiple_of(places[1, k], 128), span)
        late = places[0, k] != 0
        lhs = jnp.where(late, second[:, :, at], first[:, :, at]).reshape(4 * rows, span)
        total = total + dot(lhs, shards[k][...], ((1,), (1,)))
    p = total[:rows] + total[rows : 2 * rows] + total[2 * rows : 3 * rows] + total[3 * rows :]
    out[...] = jnp.concatenate([p, jnp.zeros((rows, 128 - rank), f32)], axis=1)


def p_of(places, shards, first, second):
    vmem = pl.BlockSpec(memory_space=pltpu.VMEM)
    return pl.pallas_call(
        p_kernel,
        out_shape=jax.ShapeDtypeStruct((first.shape[1], 128), f32),
        in_specs=[pl.BlockSpec(memory_space=pltpu.SMEM)] + [vmem] * 10,
        out_specs=vmem,
        compiler_params=pltpu.CompilerParams(vmem_limit_bytes=32 * 2**20),
        cost_estimate=pl.CostEstimate(flops=2**27, bytes_accessed=3 * 2**20, transcendentals=0),
        name="p_kernel",
    )(places, *shards, first, second)


def inverse_factor(gram):
    n = gram.shape[0]
    row = lax.broadcasted_iota(jnp.int32, (n, 2 * n), 0)
    col = lax.broadcasted_iota(jnp.int32, (n, 2 * n), 1)
    a = jnp.concatenate([gram, gram], axis=1)
    a = jnp.where(col < n, a, jnp.where(col == row + n, 1.0, 0.0))
    rows = lax.broadcasted_iota(jnp.int32, (n, 1), 0)
    scale = jnp.zeros((n, 1), f32)
    for j in range(0, n, 4):
        r = [a[j + i : j + i + 1, :] for i in range(4)]
        c = [jnp.broadcast_to(a[:, j + i : j + i + 1], (n, 2 * n)) for i in range(4)]
        g = [[jnp.broadcast_to(r[i][:, j + k : j + k + 1], (1, 2 * n)) for k in range(4)] for i in range(4)]
        for i in range(4):
            inv = 1.0 / g[i][i]
            scale = jnp.where(rows == j + i, g[i][i][:, :1], scale)
            rs = r[i] * inv
            for k in range(i + 1, 4):
                f = g[i][k] * inv
                r[k] = r[k] - f * r[i]
                c[k] = c[k] - f * c[i]
                for l in range(k, 4):
                    g[k][l] = g[k][l] - f * g[i][l]
            a = a - jnp.where(row > j + i, c[i], 0.0) * rs
    return a[:, n:] * (1.0 / jnp.sqrt(scale))


def mid_kernel(came, q_out, approx_out):
    rank, span = q_out.shape
    p = came[:, 256 : 256 + rank].astype(f32) + came[:, 256 + rank :].astype(f32)
    inverse = inverse_factor(dot(p, p, ((0,), (0,)), HIGHEST))
    p_orth = dot(p, inverse, ((1,), (1,)), HIGHEST).astype(bf16)
    q_t = dot(p_orth, came[:, :span], ((0,), (0,))) / REPS
    q_out[...] = q_t
    q_high = q_t.astype(bf16)
    q_low = (q_t - q_high.astype(f32)).astype(bf16)
    approx = dot(p_orth, q_high, ((1,), (0,))) + dot(p_orth, q_low, ((1,), (0,)))
    approx_out[...] = approx.astype(bf16)


def middle(came, span):
    vmem = pl.BlockSpec(memory_space=pltpu.VMEM)
    rows = came.shape[0]
    return pl.pallas_call(
        mid_kernel,
        out_shape=(
            jax.ShapeDtypeStruct((64, span), f32),
            jax.ShapeDtypeStruct((rows, span), bf16),
        ),
        in_specs=[vmem],
        out_specs=(vmem, vmem),
        compiler_params=pltpu.CompilerParams(vmem_limit_bytes=32 * 2**20),
        cost_estimate=pl.CostEstimate(flops=2**33, bytes_accessed=2**20, transcendentals=0),
        name="mid_kernel",
    )(came)


def body(delta, q_start, first_moment, second_moment):
    own = delta[0]
    rows, cols = own.shape
    rank = q_start.shape[1]
    wide = cols // 4
    block = cols // REPS
    narrow = block // 32
    y = lax.axis_index("y")
    zh = lax.axis_index("zh")

    x, c = lax.axis_index("x"), lax.axis_index("c")

    def along_y(a):
        return lax.all_to_all(a, "y", 0, 0, tiled=True)

    give, keep = split(zh, own)

    with jax.named_scope("q_z"):
        q_t = q_start.T
        quarter = rank // 4
        shard = jnp.concatenate(
            [
                lax.ppermute(
                    q_t[quarter * s : quarter * (s + 1)],
                    ("y", "zl"),
                    [(a * 4 + b, b * 4 + (a ^ s)) for a in range(4) for b in range(4)],
                )
                for s in range(4)
            ],
            axis=0,
        )
    with jax.named_scope("delta_give"):
        give = along_y(give)
    shard, give, keep = lax.optimization_barrier((shard, give, keep))
    with jax.named_scope("q_x"):
        shards = [shard] + [swap(shard, "x", k) for k in (1, 3, 2)]
    with jax.named_scope("delta_keep"):
        keep = along_y(keep)
    with jax.named_scope("sums_give"):
        vals = give.astype(f32)
        sums = jnp.stack([jnp.sum(vals, axis=0), jnp.sum(jnp.square(vals), axis=0)]).astype(bf16)
    with jax.named_scope("sums_zh"):
        d_came, s_came = swap(sums, "zh", 1)
    shards, keep = lax.optimization_barrier((shards, keep))
    with jax.named_scope("q_c"):
        shards = shards + [swap(s, "c", 1) for s in shards]
    with jax.named_scope("p_part"):
        at = [((x ^ k) * 2 + (c ^ i)) * (wide // 8) for i in (0, 1) for k in (0, 1, 3, 2)]
        late = [jnp.where(a >= block, 1, 0) == zh for a in at]
        places = jnp.stack([jnp.stack(late).astype(jnp.int32), jnp.stack(at) % block])
        p_part = p_of(places, shards, give, keep)
    with jax.named_scope("sums_keep"):
        vals = keep.astype(f32)
        d_keep = jnp.sum(vals, axis=0)
        s_keep = jnp.sum(jnp.square(vals), axis=0)

    with jax.named_scope("p_y"):
        p_part = p_part + (swap(p_part, "y", 1) + swap(p_part, "y", 3)) + swap(p_part, "y", 2)
    with jax.named_scope("p_zh"):
        p_part = p_part + swap(p_part, "zh", 1)
        p_part, d_came = lax.optimization_barrier((p_part, d_came))
    with jax.named_scope("send"):
        d_rows = (d_keep + d_came.astype(f32)).astype(bf16)
        d_rows = d_rows.reshape(rows, 32, narrow).transpose(1, 0, 2)
        d_rows = jnp.pad(d_rows, ((0, 0), (0, 0), (0, 256 - narrow)))
        p_rows = p_part[:, :rank]
        high = lax.reduce_precision(p_rows, 8, 7)
        p_rows = jnp.concatenate([high, p_rows - high], axis=1).astype(bf16)
        p_rows = jnp.broadcast_to(p_rows[None], (32, rows, 2 * rank))
        came = lax.all_to_all(jnp.concatenate([d_rows, p_rows], axis=2), ROW, 0, 0, tiled=True)
    with jax.named_scope("second"):
        mean_square = (s_keep + s_came.astype(f32)) / REPS
        new_second = beta_second * second_moment + (1.0 - beta_second) * mean_square
        below = jnp.sqrt(new_second * fix_second) + epsilon
        came, new_second, below = lax.optimization_barrier((came, new_second, below))
    with jax.named_scope("middle"):
        q_t, approx_cols = middle(came.reshape(32 * rows, 256 + 2 * rank), narrow)
        q_new = q_t.T
    with jax.named_scope("approx"):
        approx = lax.all_to_all(
            approx_cols.reshape(32, rows, narrow), ROW, 0, 0, tiled=True
        )
        approx = approx.transpose(1, 0, 2).reshape(rows, block).astype(f32)

    new_first = beta_first * first_moment + (1.0 - beta_first) * approx
    update = new_first * fix_first / below
    return (update, new_first, new_second, q_new)


def solution(mesh):
    fine = Mesh(mesh.devices.reshape(SIZES), NAMES)
    in_specs = (P(REP, ROW, None), P(ROW, None), P(ROW, REP), P(ROW, REP))
    out_specs = (P(ROW, REP), P(ROW, REP), P(ROW, REP), P(REP + ROW, None))
    return jax.shard_map(body, mesh=fine, in_specs=in_specs, out_specs=out_specs, check_vma=False)
```
